32 devices in a mesh: group: 2 (over y), walker: 4 (over z), param: 4 (over x, core).
Axes of the slice: x: 2, y: 2, z: 4, core: 2. Of those that a mesh axis runs over, the one named last changes fastest.
Arguments:
- activations: bfloat16 [96, 1024, 256], P(('group', 'walker'), 'param'), parts along dimension 0, may hold values from -6 to 6
- cotangents: bfloat16 [96, 1024, 1024], P(('group', 'walker'), 'param'), parts along dimension 0, may hold values from -0.0010036526 to 0.0010036526
- local_energy: float32 [96], P(('group', 'walker')), parts along dimension 0, may hold values from -6 to 6
- walker_ids: int32 [96], P(('group', 'walker')), parts along dimension 0, may hold values from 0 to 47, each once
- prev_direction: float32 [512, 1024], P('group', 'param'), parts along dimension 0, may hold values from -6 to 6
- column_order: int32 [2048], P('group'), parts along dimension 0, may hold values from 0 to 1023, each once
- weights: float32 [512, 1024], P('group', 'param'), parts along dimension 0, may hold values from -0.375 to 0.375
Outputs:
- direction: float32 [512, 1024], P('group', 'param'), parts along dimension 0
- new_weights: float32 [512, 1024], P('group', 'param'), parts along dimension 0
- coefficients: float32 [96], P(('group', 'walker')), parts along dimension 0
The draws below stay inside these ranges and needn't reach their ends.
There are 2 independent parts, one for each index of `group`. The reference program is written for one: setup_inputs(seed, part) draws one part's arguments, and reference() takes and returns one part's arrays. A program takes and returns all parts, laid end to end along the dimension named above; each array names one. Nothing has to cross between parts.
Inputs may be any that keep to these rules, and one draw needn't show every extreme that they name: `walker_ids`: each walker id appears once. `column_order`: each column appears once.
All inputs are finite; a program needn't handle non-finite values.
Results may differ from the reference program's by a relative error of at most 0.0015.
Values may be sent and summed in bfloat16 or wider, within the bound.
A program may use at most 128 MiB of HBM per device.

```python
import jax
import jax.numpy as jnp
from jax import lax

D_IN = 256
ORB = 1024
ELEC = 1024
WALKERS = 48


def draw_activations(key, part):
    common = jnp.clip(jax.random.normal(jax.random.fold_in(key, 101), (ELEC, D_IN), jnp.float32), -4.0, 4.0)
    private = jnp.clip(jax.random.normal(jax.random.fold_in(key, 102), (WALKERS, ELEC, D_IN), jnp.float32), -4.0, 4.0)
    summed = jnp.clip(common[None, :, :] + private, -6.0, 6.0)
    return summed.astype(jnp.bfloat16)


def draw_cotangents(key, part):
    factor_scale = (10.0 * D_IN * ORB * ELEC) ** (-0.5)
    walker_loads = jnp.clip(jax.random.normal(jax.random.fold_in(key, 201), (WALKERS, 4), jnp.float32), -3.0, 3.0)
    summed = jnp.clip(jax.random.normal(jax.random.fold_in(key, 202), (WALKERS, ORB, ELEC), jnp.float32), -4.0, 4.0)
    for shared_index in range(4):
        shared_key = jax.random.fold_in(key, 300 + shared_index)
        shared_part = jnp.clip(jax.random.normal(shared_key, (ORB, ELEC), jnp.float32), -4.0, 4.0)
        summed = summed + walker_loads[:, shared_index, None, None] * shared_part[None, :, :]
    return (factor_scale * summed).astype(jnp.bfloat16)


def level_of(rng, dims, shards, smallest, largest):
    def one(position, parts):
        steps = jax.random.uniform(jax.random.fold_in(jax.random.fold_in(rng, 6), position), (parts,), jnp.float32, smallest / len(shards), largest / len(shards))
        return jnp.repeat(jnp.exp(steps), dims[position] // parts).reshape((-1,) + (1,) * (len(dims) - position - 1))

    factor_of = one(*shards[0])
    for cut in shards[1:]:
        factor_of = factor_of * one(*cut)
    return factor_of


def bell_draw(stream_key, extent, deviation, bound, pieces=(), kind=jnp.bfloat16):
    loudness = level_of(stream_key, extent, pieces, -0.22, 0.18) if pieces else 1.0
    entries = jax.random.normal(stream_key, extent, jnp.float32) * deviation * loudness
    return jnp.minimum(jnp.maximum(entries, -bound), bound).astype(kind)


def setup_inputs(seed: int = 0, part: int = 0) -> dict:
    seeds = jax.random.split(jax.random.key(seed), 8)
    own_keys = jax.random.split(jax.random.fold_in(seeds[7], part), 8)
    return {
        "activations": draw_activations(jax.random.fold_in(jax.random.fold_in(seeds[7], part), 71), part),
        "cotangents": draw_cotangents(jax.random.fold_in(jax.random.fold_in(seeds[7], part), 71), part),
        "local_energy": bell_draw(own_keys[2], (WALKERS,), 1.0, 6.0, ((0, 4),), jnp.float32),
        "walker_ids": jax.random.permutation(own_keys[3], WALKERS).astype(jnp.int32),
        "prev_direction": bell_draw(own_keys[4], (D_IN, ORB), 0.5, 6.0, ((1, 4),), jnp.float32),
        "column_order": jax.random.permutation(own_keys[5], ORB).astype(jnp.int32),
        "weights": bell_draw(own_keys[6], (D_IN, ORB), D_IN ** -0.5, 0.375, ((1, 4),), jnp.float32),
    }


def solve_system(system, zeta):
    factor = jnp.linalg.cholesky(system)
    column = zeta[:, None]
    middle = lax.linalg.triangular_solve(factor, column, left_side=True, lower=True, transpose_a=False)
    result = lax.linalg.triangular_solve(factor, middle, left_side=True, lower=True, transpose_a=True)
    return result[:, 0]

def reference(activations, cotangents, local_energy, walker_ids, prev_direction, column_order, weights):

    def one_walker(pair):
        feats, cots = pair
        return lax.dot_general(feats.astype(jnp.float32), cots.astype(jnp.float32), (((0,), (1,)), ((), ())), preferred_element_type=jnp.float32)
    grads = lax.map(one_walker, (activations, cotangents)).reshape(WALKERS, D_IN * ORB)
    centered = (grads - jnp.mean(grads, axis=0)).astype(jnp.bfloat16)
    gram = jnp.dot(centered.astype(jnp.float32), centered.T.astype(jnp.float32), preferred_element_type=jnp.float32)
    aligned = prev_direction[:, column_order]
    wide = centered.astype(jnp.float32)
    projections = jnp.dot(wide, aligned.reshape(-1), precision=lax.Precision.HIGHEST)
    centered_energy = local_energy[walker_ids] - jnp.mean(local_energy)
    zeta = centered_energy - 0.9 * projections
    system = gram + 0.002 * jnp.eye(WALKERS, dtype=jnp.float32) + 1.0 / WALKERS
    coefficients = solve_system(system, zeta)
    direction = jnp.dot(coefficients, wide, precision=lax.Precision.HIGHEST).reshape(D_IN, ORB) + 0.9 * aligned
    return (direction, weights - 0.05 * direction, coefficients)
```

```python
import functools

import jax
import jax.numpy as jnp
from jax import lax
from jax.experimental import pallas as pl
from jax.experimental.pallas import tpu as pltpu
from jax.sharding import PartitionSpec as P

F32 = jnp.float32
BF16 = jnp.bfloat16
MESH = pl.DeviceIdType.MESH


def solve_system(system, zeta):
    factor = jnp.linalg.cholesky(system)
    column = zeta[:, None]
    middle = lax.linalg.triangular_solve(
        factor, column, left_side=True, lower=True, transpose_a=False
    )
    result = lax.linalg.triangular_solve(
        factor, middle, left_side=True, lower=True, transpose_a=True
    )
    return result[:, 0]


def plain_shards(
    activations, cotangents, local_energy, walker_ids, prev_direction, column_order, weights
):
    rows = cotangents.shape[0]
    orb_local = cotangents.shape[1]
    width_in = activations.shape[2]
    walkers = rows * lax.axis_size("walker")
    walker_pos = lax.axis_index("walker")
    param_pos = lax.axis_index("param")
    grads = jnp.einsum(
        "wnd,won->wdo",
        lax.all_gather(activations, "param", axis=1, tiled=True),
        cotangents,
        preferred_element_type=jnp.float32,
    )
    flat = grads.reshape(rows, width_in * orb_local)
    column_total = lax.psum(jnp.sum(flat, axis=0), "walker")
    centered = (flat - column_total / walkers).astype(jnp.bfloat16)
    energies_all = lax.all_gather(local_energy, "walker", axis=0, tiled=True)
    energy_mean = jnp.mean(energies_all)
    centered_energy = energies_all[walker_ids] - energy_mean
    stored = lax.all_gather(prev_direction, "param", axis=1, tiled=True)
    my_order = lax.dynamic_slice_in_dim(column_order, param_pos * orb_local, orb_local)
    aligned = jnp.take(stored, my_order, axis=1)
    wide = centered.astype(jnp.float32)
    proj_part = jnp.dot(wide, aligned.reshape(-1), precision=lax.Precision.HIGHEST)
    block = lax.dot_general(
        centered,
        lax.all_gather(centered, "walker", axis=0, tiled=True),
        (((1,), (1,)), ((), ())),
        preferred_element_type=jnp.float32,
    )
    gram_mine, proj_mine = lax.psum((block, proj_part), "param")
    zeta_mine = centered_energy - 0.9 * proj_mine
    gram, zeta = (
        lax.all_gather(gram_mine, "walker", axis=0, tiled=True),
        lax.all_gather(zeta_mine, "walker", axis=0, tiled=True),
    )
    system = gram + 0.002 * jnp.eye(walkers, dtype=jnp.float32) + 1.0 / walkers
    solved = solve_system(system, zeta)
    mine = lax.dynamic_slice_in_dim(solved, walker_pos * rows, rows)
    update_part = jnp.dot(mine, wide, precision=lax.Precision.HIGHEST)
    update_total = lax.psum(update_part, "walker")
    direction = update_total.reshape(width_in, orb_local) + 0.9 * aligned
    return (direction, weights - 0.05 * direction, mine)


def kernel(
    act, cot, prev, order, weights, packed,
    dir_out, w_out, coef_out,
    agath, cbuf, sbuf, rbuf, run, runs, total, cent, stored, alig, mean_ref,
    gred, zred, gsum, dscr, ebuf, esort, csol,
    loc_sem, xs, xr, bs, br, fs, fr, zs, zr, ps, pr, gs, gr, hs, hr, ds, dr, es, er,
    *, Z, PP,
):
    R, n, D = act.shape
    O = cot.shape[1]
    W = R * Z
    X = PP // 2
    dc = D // Z
    L = gsum.shape[1]
    halves = O // 128
    z = lax.axis_index("walker")
    p = lax.axis_index("param")
    x = p // 2
    c = p % 2
    sib = x * 2 + (1 - c)

    def xpeer(j):
        return lax.rem(x + j, X) * 2 + c

    def remote(src, dst, ssem, rsem, axis, idx):
        return pltpu.make_async_remote_copy(
            src_ref=src, dst_ref=dst, send_sem=ssem, recv_sem=rsem,
            device_id={axis: idx}, device_id_type=MESH,
        )

    def cot_copy(r):
        return pltpu.make_async_copy(cot.at[r], cbuf.at[r], loc_sem.at[0, r])

    def act_copy(r):
        return pltpu.make_async_copy(
            act.at[r], agath.at[r, pl.ds(pl.multiple_of(p * n, n), n)], loc_sem.at[1, r]
        )

    def rows_of(q):
        return pl.ds(pl.multiple_of(q * n, n), n)

    def x_send(r, j):
        return remote(act.at[r], agath.at[r, rows_of(p)], xs.at[r, j], xr.at[r, x], "param", xpeer(j))

    def x_recv(r, j):
        q = xpeer(j)
        return remote(act.at[r], agath.at[r, rows_of(q)], xs.at[r, j], xr.at[r, q // 2], "param", q)

    def b_send(r):
        return remote(act.at[r], agath.at[r, rows_of(p)], bs.at[r], br.at[r], "param", sib)

    def b_recv(r):
        return remote(act.at[r], agath.at[r, rows_of(sib)], bs.at[r], br.at[r], "param", sib)

    def f_send(r, j):
        q = xpeer(j)
        return remote(
            agath.at[r, rows_of(q)], agath.at[r, rows_of(q)], fs.at[r, j], fr.at[r, j], "param", sib
        )

    def f_recv(r, j):
        q = lax.rem(x + j, X) * 2 + (1 - c)
        return remote(
            agath.at[r, rows_of(q)], agath.at[r, rows_of(q)], fs.at[r, j], fr.at[r, j], "param", sib
        )

    def chunk(q):
        return pl.ds(pl.multiple_of(q * dc, dc), dc)

    def z_send(i, k):
        q = lax.rem(z + k, Z)
        return remote(sbuf.at[i, chunk(q)], rbuf.at[z, i], zs.at[i, k], zr.at[i, z], "walker", q)

    def z_recv(i, k):
        q = lax.rem(z + k, Z)
        return remote(sbuf.at[i, chunk(q)], rbuf.at[q, i], zs.at[i, k], zr.at[i, q], "walker", q)

    def p_send(j):
        q = lax.rem(p + j, PP)
        return remote(prev.at[chunk(z)], stored.at[p], ps.at[j], pr.at[p], "param", q)

    def p_recv(j):
        q = lax.rem(p + j, PP)
        return remote(prev.at[chunk(z)], stored.at[q], ps.at[j], pr.at[q], "param", q)

    def g_send(j):
        q = lax.rem(p + j, PP)
        return remote(gsum, gred.at[p], gs.at[j], gr.at[p], "param", q)

    def g_recv(j):
        q = lax.rem(p + j, PP)
        return remote(gsum, gred.at[q], gs.at[j], gr.at[q], "param", q)

    def h_send(k):
        q = lax.rem(z + k, Z)
        return remote(zred.at[z], zred.at[z], hs.at[k], hr.at[z], "walker", q)

    def h_recv(k):
        q = lax.rem(z + k, Z)
        return remote(zred.at[q], zred.at[q], hs.at[k], hr.at[q], "walker", q)

    def d_send(k):
        q = lax.rem(z + k, Z)
        return remote(dscr.at[chunk(z)], dscr.at[chunk(z)], ds.at[k], dr.at[z], "walker", q)

    def d_recv(k):
        q = lax.rem(z + k, Z)
        return remote(dscr.at[chunk(q)], dscr.at[chunk(q)], ds.at[k], dr.at[q], "walker", q)

    def e_send(k):
        q = lax.rem(z + k, Z)
        return remote(packed, ebuf.at[z], es.at[k], er.at[z], "walker", q)

    def e_recv(k):
        q = lax.rem(z + k, Z)
        return remote(packed, ebuf.at[q], es.at[k], er.at[q], "walker", q)

    barrier = pltpu.get_barrier_semaphore()
    for j in range(1, PP):
        pl.semaphore_signal(barrier, inc=1, device_id={"param": lax.rem(p + j, PP)}, device_id_type=MESH)
    for k in range(1, Z):
        pl.semaphore_signal(barrier, inc=1, device_id={"walker": lax.rem(z + k, Z)}, device_id_type=MESH)

    def start_local(r, _):
        cot_copy(r).start()
        act_copy(r).start()
        return 0

    lax.fori_loop(0, R, start_local, 0)
    pl.semaphore_wait(barrier, PP + Z - 2)

    def start_sends(r, _):
        for j in range(1, X):
            x_send(r, j).start()
        b_send(r).start()
        return 0

    lax.fori_loop(0, R, start_sends, 0)
    for k in range(1, Z):
        e_send(k).start()
    for j in range(1, PP):
        p_send(j).start()

    def forward(r):
        for j in range(1, X):
            x_recv(r, j).wait_recv()
            f_send(r, j).start()

    def grads_of(r):
        cot_copy(r).wait()
        act_copy(r).wait()
        b_recv(r).wait_recv()
        for j in range(1, X):
            f_recv(r, j).wait_recv()
        flipped = jnp.dot(cbuf[r], agath[r], preferred_element_type=F32)
        return flipped.T

    def send_row(i):
        rbuf[z, i] = sbuf[i, chunk(z), :]
        for k in range(1, Z):
            z_send(i, k).start()

    def first():
        g = grads_of(0)
        high = g.astype(BF16)
        low = (g - high.astype(F32)).astype(BF16)
        sbuf[0] = high
        sbuf[R] = low
        run[...] = high.astype(F32) + low.astype(F32)
        send_row(0)
        send_row(R)

    def inverse(r):
        return 1.0 / jnp.asarray(r, F32)

    def later(r):
        g = grads_of(r)
        middle = run[...] * inverse(r)
        step = (g - middle).astype(BF16)
        sbuf[r] = step
        run[...] += middle + step.astype(F32)
        send_row(r)

    forward(0)
    forward(1)
    first()

    def body(r, _):
        forward(r)
        later(r - 1)
        return 0

    lax.fori_loop(2, R, body, 0)
    later(R - 1)

    for j in range(1, PP):
        p_recv(j).wait_recv()
    stored[p] = prev[chunk(z), :]
    mine = order[:, pl.ds(pl.multiple_of(p * O, O), O)]
    acc = jnp.zeros((3 * dc, O), F32)
    for q in range(PP):
        hot = (lax.broadcasted_iota(jnp.int32, (O, O), 0) + q * O == mine).astype(F32).astype(BF16)
        s = stored[q]
        s1 = s.astype(BF16)
        rest = s - s1.astype(F32)
        s2 = rest.astype(BF16)
        s3 = (rest - s2.astype(F32)).astype(BF16)
        acc += jnp.dot(jnp.concatenate([s1, s2, s3], axis=0), hot, preferred_element_type=F32)
    alig[...] = acc[:dc] + (acc[dc : 2 * dc] + acc[2 * dc :])

    for k in range(1, Z):
        e_recv(k).wait_recv()
    ebuf[z] = packed[...]
    lane = lax.broadcasted_iota(jnp.int32, (R, 128), 1)
    energy_sum = jnp.zeros((1, 1), F32)
    for q in range(Z):
        energy_sum += jnp.sum(ebuf[q, R : R + 1, :], axis=1, keepdims=True)
    energy_mean = energy_sum / W
    for q in range(Z):
        ids = ebuf[q, 0:R, :]
        picked = jnp.zeros((R, 128), F32)
        for s in range(Z):
            hit = (ids == (lane + s * R).astype(F32)) & (lane < R)
            picked += jnp.where(hit, ebuf[s, R : R + 1, :], 0.0)
        value = jnp.sum(picked, axis=1, keepdims=True) - energy_mean
        esort[q * R : (q + 1) * R, :] = jnp.broadcast_to(value, (R, 128))

    for k in range(1, Z):
        z_recv(0, k).wait_recv()
        z_recv(R, k).wait_recv()

    def put(q, r, g):
        for h in range(halves):
            cent[h, pl.ds(pl.multiple_of((q * R + r) * dc, dc), dc), :] = g[:, h * 128 : (h + 1) * 128]

    for q in range(Z):
        g = rbuf[q, 0].astype(F32) + rbuf[q, R].astype(F32)
        runs[q] = g
        put(q, 0, g)

    def rebuild(r, _):
        for k in range(1, Z):
            z_recv(r, k).wait_recv()
        for q in range(Z):
            middle = runs[q] * inverse(r)
            g = middle + rbuf[q, r].astype(F32)
            put(q, r, g)
            runs[q] += g
        return 0

    lax.fori_loop(1, R, rebuild, 0)
    acc = runs[0]
    for q in range(1, Z):
        acc += runs[q]
    mean_ref[...] = acc * (1.0 / W)

    def gram_step(i, carry):
        gram, proj = carry
        parts = []
        for u in range(4):
            d = i * 4 + u
            row = jnp.concatenate(
                [cent[h, pl.ds(d, W, stride=dc), :] for h in range(halves)], axis=1
            )
            row = row - mean_ref[pl.ds(d, 1), :]
            proj = proj + row * alig[pl.ds(d, 1), :]
            parts.append(row.astype(BF16))
        wide = jnp.concatenate(parts, axis=1)
        gram = gram + lax.dot_general(
            wide, wide, (((1,), (1,)), ((), ())), preferred_element_type=F32
        )
        return gram, proj

    gram, proj = lax.fori_loop(
        0, dc // 4, gram_step, (jnp.zeros((W, W), F32), jnp.zeros((W, O), F32))
    )
    gsum[...] = jnp.zeros((W, L), F32)
    gsum[:, 0:W] = gram
    gsum[:, W : W + 1] = jnp.sum(proj, axis=1, keepdims=True)
    for j in range(1, PP):
        g_send(j).start()
    gred[p] = gsum[...]
    for j in range(1, PP):
        g_recv(j).wait_recv()
    acc = gred[0]
    for q in range(1, PP):
        acc += gred[q]
    zred[z] = acc
    for k in range(1, Z):
        h_send(k).start()
    for k in range(1, Z):
        h_recv(k).wait_recv()
    acc = zred[0]
    for q in range(1, Z):
        acc += zred[q]

    sub = lax.broadcasted_iota(jnp.int32, (W, L), 0)
    col = lax.broadcasted_iota(jnp.int32, (W, L), 1)
    damp = jnp.where(sub == col, 0.002, 0.0) + 1.0 / W
    zeta = esort[:, 0:1] - 0.9 * acc[:, W : W + 1]
    m = jnp.where(col == W, zeta, acc + damp)
    for k in range(W):
        pivot_row = m[k : k + 1, :]
        pivot_row = pivot_row / pivot_row[:, k : k + 1]
        m = jnp.where(sub == k, pivot_row, m - m[:, k : k + 1] * pivot_row)
    solved = jnp.broadcast_to(m[:, W : W + 1], (W, 128))
    csol[...] = solved
    sub = lax.broadcasted_iota(jnp.int32, (W, 128), 0)
    col = lax.broadcasted_iota(jnp.int32, (W, 128), 1)
    coef_out[...] = jnp.sum(jnp.where(sub == col + z * R, solved, 0.0), axis=0, keepdims=True)

    for h in range(halves):
        cols = slice(h * 128, (h + 1) * 128)
        mean_half = mean_ref[:, cols]

        def add(w, acc):
            part = cent[h, pl.ds(pl.multiple_of(w * dc, dc), dc), :] - mean_half
            return acc + csol[pl.ds(w, 1), :] * part

        acc = lax.fori_loop(0, W, add, jnp.zeros((dc, 128), F32), unroll=4)
        dscr[chunk(z), cols] = acc + 0.9 * alig[:, cols]
    for k in range(1, Z):
        d_send(k).start()
    for k in range(1, Z):
        d_recv(k).wait_recv()
    value = dscr[...]
    dir_out[...] = value
    w_out[...] = weights[...] - 0.05 * value

    def drain(r, _):
        for j in range(1, X):
            x_send(r, j).wait_send()
            f_send(r, j).wait_send()
        b_send(r).wait_send()
        return 0

    lax.fori_loop(0, R, drain, 0)

    def drain_rows(i, _):
        for k in range(1, Z):
            z_send(i, k).wait_send()
        return 0

    lax.fori_loop(0, R + 1, drain_rows, 0)
    for j in range(1, PP):
        p_send(j).wait_send()
        g_send(j).wait_send()
    for k in range(1, Z):
        e_send(k).wait_send()
        h_send(k).wait_send()
        d_send(k).wait_send()


def fused_shards(
    activations, cotangents, local_energy, walker_ids, prev_direction, column_order, weights
):
    R, n, D = activations.shape
    O, N = cotangents.shape[1:]
    Z = lax.axis_size("walker")
    PP = lax.axis_size("param")
    X = PP // 2
    W = R * Z
    dc = D // Z
    L = -(-(W + 1) // 128) * 128
    rp = -(-(R + 1) // 8) * 8
    packed = jnp.zeros((rp, 128), F32)
    packed = packed.at[:R, :].set(jnp.broadcast_to(walker_ids.astype(F32)[:, None], (R, 128)))
    packed = packed.at[R, :R].set(local_energy)
    vmem = pl.BlockSpec(memory_space=pltpu.VMEM)
    hbm = pl.BlockSpec(memory_space=pl.ANY)
    dma = pltpu.SemaphoreType.DMA
    direction, new_weights, coef = pl.pallas_call(
        functools.partial(kernel, Z=Z, PP=PP),
        out_shape=(
            jax.ShapeDtypeStruct((D, O), F32),
            jax.ShapeDtypeStruct((D, O), F32),
            jax.ShapeDtypeStruct((1, 128), F32),
        ),
        in_specs=[hbm, hbm, vmem, vmem, vmem, vmem],
        out_specs=(vmem, vmem, vmem),
        scratch_shapes=[
            pltpu.VMEM((R, N, D), BF16),
            pltpu.VMEM((R, O, N), BF16),
            pltpu.VMEM((R + 1, D, O), BF16),
            pltpu.VMEM((Z, R + 1, dc, O), BF16),
            pltpu.VMEM((D, O), F32),
            pltpu.VMEM((Z, dc, O), F32),
            pltpu.VMEM((dc, O), F32),
            pltpu.VMEM((O // 128, W * dc, 128), F32),
            pltpu.VMEM((PP, dc, O), F32),
            pltpu.VMEM((dc, O), F32),
            pltpu.VMEM((dc, O), F32),
            pltpu.VMEM((PP, W, L), F32),
            pltpu.VMEM((Z, W, L), F32),
            pltpu.VMEM((W, L), F32),
            pltpu.VMEM((D, O), F32),
            pltpu.VMEM((Z, rp, 128), F32),
            pltpu.VMEM((W, 128), F32),
            pltpu.VMEM((W, 128), F32),
            dma((2, R)),
            dma((R, X)), dma((R, X)),
            dma((R,)), dma((R,)),
            dma((R, X)), dma((R, X)),
            dma((R + 1, Z)), dma((R + 1, Z)),
            dma((PP,)), dma((PP,)),
            dma((PP,)), dma((PP,)),
            dma((Z,)), dma((Z,)),
            dma((Z,)), dma((Z,)),
            dma((Z,)), dma((Z,)),
        ],
        compiler_params=pltpu.CompilerParams(
            collective_id=0, has_side_effects=True, vmem_limit_bytes=48 * 1024 * 1024
        ),
        cost_estimate=pl.CostEstimate(
            flops=2 * R * D * O * N, bytes_accessed=2 * R * N * (D + O), transcendentals=0
        ),
    )(activations, cotangents, prev_direction, column_order.reshape(1, -1), weights, packed)
    return (direction, new_weights, coef[0, :R])


def shards(*args):
    R, n, D = args[0].shape
    O = args[1].shape[1]
    Z = lax.axis_size("walker")
    fits = O % 128 == 0 and D % (16 * Z) == 0 and R * Z <= 120 and R >= 3 and n % 16 == 0
    if fits and lax.axis_size("param") % 2 == 0:
        return fused_shards(*args)
    return plain_shards(*args)


def solution(mesh):
    in_specs = (
        P(("group", "walker"), "param", None),
        P(("group", "walker"), "param", None),
        P(("group", "walker")),
        P(("group", "walker")),
        P("group", "param"),
        P("group"),
        P("group", "param"),
    )
    out_specs = (P("group", "param"), P("group", "param"), P(("group", "walker")))
    return jax.shard_map(shards, mesh=mesh, in_specs=in_specs, out_specs=out_specs, check_vma=False)
```

```python
import functools

import jax
import jax.numpy as jnp
from jax import lax
from jax.experimental import pallas as pl
from jax.experimental.pallas import tpu as pltpu
from jax.sharding import PartitionSpec as P

F32 = jnp.float32
BF16 = jnp.bfloat16
MESH = pl.DeviceIdType.MESH
WINDOW = 2


def solve_system(system, zeta):
    factor = jnp.linalg.cholesky(system)
    column = zeta[:, None]
    middle = lax.linalg.triangular_solve(
        factor, column, left_side=True, lower=True, transpose_a=False
    )
    result = lax.linalg.triangular_solve(
        factor, middle, left_side=True, lower=True, transpose_a=True
    )
    return result[:, 0]


def plain_shards(
    activations, cotangents, local_energy, walker_ids, prev_direction, column_order, weights
):
    rows = cotangents.shape[0]
    orb_local = cotangents.shape[1]
    width_in = activations.shape[2]
    walkers = rows * lax.axis_size("walker")
    walker_pos = lax.axis_index("walker")
    param_pos = lax.axis_index("param")
    grads = jnp.einsum(
        "wnd,won->wdo",
        lax.all_gather(activations, "param", axis=1, tiled=True),
        cotangents,
        preferred_element_type=jnp.float32,
    )
    flat = grads.reshape(rows, width_in * orb_local)
    column_total = lax.psum(jnp.sum(flat, axis=0), "walker")
    centered = (flat - column_total / walkers).astype(jnp.bfloat16)
    energies_all = lax.all_gather(local_energy, "walker", axis=0, tiled=True)
    energy_mean = jnp.mean(energies_all)
    centered_energy = energies_all[walker_ids] - energy_mean
    stored = lax.all_gather(prev_direction, "param", axis=1, tiled=True)
    my_order = lax.dynamic_slice_in_dim(column_order, param_pos * orb_local, orb_local)
    aligned = jnp.take(stored, my_order, axis=1)
    wide = centered.astype(jnp.float32)
    proj_part = jnp.dot(wide, aligned.reshape(-1), precision=lax.Precision.HIGHEST)
    block = lax.dot_general(
        centered,
        lax.all_gather(centered, "walker", axis=0, tiled=True),
        (((1,), (1,)), ((), ())),
        preferred_element_type=jnp.float32,
    )
    gram_mine, proj_mine = lax.psum((block, proj_part), "param")
    zeta_mine = centered_energy - 0.9 * proj_mine
    gram, zeta = (
        lax.all_gather(gram_mine, "walker", axis=0, tiled=True),
        lax.all_gather(zeta_mine, "walker", axis=0, tiled=True),
    )
    system = gram + 0.002 * jnp.eye(walkers, dtype=jnp.float32) + 1.0 / walkers
    solved = solve_system(system, zeta)
    mine = lax.dynamic_slice_in_dim(solved, walker_pos * rows, rows)
    update_part = jnp.dot(mine, wide, precision=lax.Precision.HIGHEST)
    update_total = lax.psum(update_part, "walker")
    direction = update_total.reshape(width_in, orb_local) + 0.9 * aligned
    return (direction, weights - 0.05 * direction, mine)


def kernel(
    act, cot, prev_in, order_in, energy_in, ids_in,
    dir_out, coef_out,
    agath, cbuf, sbuf, rbuf, run, runs, total, cent, stored, alig, mean_ref,
    gred, zred, gsum, dscr, ebuf, esort, csol, prev, order, energy, ids_ref, packed,
    loc_sem, in_sem, xs, xr, bs, br, fs, fr, zs, zr, ps, pr, pbs, pbr, pfs, pfr, gs, gr, hs, hr, ds, dr, es, er,
    *, Z, PP,
):
    R, n, D = act.shape
    O = cot.shape[1]
    W = R * Z
    X = PP // 2
    dc = D // Z
    L = gsum.shape[1]
    fold = gsum.shape[0] != W
    halves = O // 128
    z = lax.axis_index("walker")
    p = lax.axis_index("param")
    x = p // 2
    c = p % 2
    sib = x * 2 + (1 - c)

    def xpeer(j):
        return lax.rem(x + j, X) * 2 + c

    def remote(src, dst, ssem, rsem, axis, idx):
        return pltpu.make_async_remote_copy(
            src_ref=src, dst_ref=dst, send_sem=ssem, recv_sem=rsem,
            device_id={axis: idx}, device_id_type=MESH,
        )

    def cot_copy(r):
        return pltpu.make_async_copy(cot.at[r], cbuf.at[r], loc_sem.at[0, r])

    def act_copy(r):
        return pltpu.make_async_copy(
            act.at[r], agath.at[r, pl.ds(pl.multiple_of(p * n, n), n)], loc_sem.at[1, r]
        )

    def rows_of(q):
        return pl.ds(pl.multiple_of(q * n, n), n)

    def x_send(r, j):
        return remote(act.at[r], agath.at[r, rows_of(p)], xs.at[r, j], xr.at[r, x], "param", xpeer(j))

    def x_recv(r, j):
        q = xpeer(j)
        return remote(act.at[r], agath.at[r, rows_of(q)], xs.at[r, j], xr.at[r, q // 2], "param", q)

    def b_send(r):
        return remote(act.at[r], agath.at[r, rows_of(p)], bs.at[r], br.at[r], "param", sib)

    def b_recv(r):
        return remote(act.at[r], agath.at[r, rows_of(sib)], bs.at[r], br.at[r], "param", sib)

    def f_send(r, j):
        q = xpeer(j)
        return remote(
            agath.at[r, rows_of(q)], agath.at[r, rows_of(q)], fs.at[r, j], fr.at[r, j], "param", sib
        )

    def f_recv(r, j):
        q = lax.rem(x + j, X) * 2 + (1 - c)
        return remote(
            agath.at[r, rows_of(q)], agath.at[r, rows_of(q)], fs.at[r, j], fr.at[r, j], "param", sib
        )

    def chunk(q):
        return pl.ds(pl.multiple_of(q * dc, dc), dc)

    def z_send(i, k):
        q = lax.rem(z + k, Z)
        return remote(sbuf.at[i, chunk(q)], rbuf.at[z, i], zs.at[i, k], zr.at[i, z], "walker", q)

    def z_recv(i, k):
        q = lax.rem(z + k, Z)
        return remote(sbuf.at[i, chunk(q)], rbuf.at[q, i], zs.at[i, k], zr.at[i, q], "walker", q)

    def p_send(j):
        return remote(prev.at[chunk(z)], stored.at[p], ps.at[j], pr.at[x], "param", xpeer(j))

    def p_recv(j):
        q = xpeer(j)
        return remote(prev.at[chunk(z)], stored.at[q], ps.at[j], pr.at[q // 2], "param", q)

    def pb_send():
        return remote(prev.at[chunk(z)], stored.at[p], pbs.at[0], pbr.at[0], "param", sib)

    def pb_recv():
        return remote(prev.at[chunk(z)], stored.at[sib], pbs.at[0], pbr.at[0], "param", sib)

    def pf_send(j):
        q = xpeer(j)
        return remote(stored.at[q], stored.at[q], pfs.at[j], pfr.at[j], "param", sib)

    def pf_recv(j):
        q = lax.rem(x + j, X) * 2 + (1 - c)
        return remote(stored.at[q], stored.at[q], pfs.at[j], pfr.at[j], "param", sib)

    def g_send(j):
        q = lax.rem(p + j, PP)
        return remote(gsum, gred.at[p], gs.at[j], gr.at[p], "param", q)

    def g_recv(j):
        q = lax.rem(p + j, PP)
        return remote(gsum, gred.at[q], gs.at[j], gr.at[q], "param", q)

    def h_send(k):
        q = lax.rem(z + k, Z)
        return remote(zred.at[z], zred.at[z], hs.at[k], hr.at[z], "walker", q)

    def h_recv(k):
        q = lax.rem(z + k, Z)
        return remote(zred.at[q], zred.at[q], hs.at[k], hr.at[q], "walker", q)

    def d_send(k):
        q = lax.rem(z + k, Z)
        return remote(dscr.at[chunk(z)], dscr.at[chunk(z)], ds.at[k], dr.at[z], "walker", q)

    def d_recv(k):
        q = lax.rem(z + k, Z)
        return remote(dscr.at[chunk(q)], dscr.at[chunk(q)], ds.at[k], dr.at[q], "walker", q)

    def e_send(k):
        q = lax.rem(z + k, Z)
        return remote(packed, ebuf.at[z], es.at[k], er.at[z], "walker", q)

    def e_recv(k):
        q = lax.rem(z + k, Z)
        return remote(packed, ebuf.at[q], es.at[k], er.at[q], "walker", q)

    barrier = pltpu.get_barrier_semaphore()
    for j in range(1, PP):
        pl.semaphore_signal(barrier, inc=1, device_id={"param": lax.rem(p + j, PP)}, device_id_type=MESH)
    for k in range(1, Z):
        pl.semaphore_signal(barrier, inc=1, device_id={"walker": lax.rem(z + k, Z)}, device_id_type=MESH)

    inputs = [
        pltpu.make_async_copy(src, dst, in_sem.at[i])
        for i, (src, dst) in enumerate(
            ((prev_in, prev), (order_in, order), (energy_in, energy), (ids_in, ids_ref))
        )
    ]
    for copy in inputs:
        copy.start()

    def start_local(r, _):
        cot_copy(r).start()
        act_copy(r).start()
        return 0

    lax.fori_loop(0, R, start_local, 0)
    pl.semaphore_wait(barrier, PP + Z - 2)

    def start_x(r):
        for j in range(1, X):
            x_send(r, j).start()

    for r in range(WINDOW):
        start_x(r)

    def start_b(r, _):
        b_send(r).start()
        return 0

    lax.fori_loop(0, R, start_b, 0)
    for copy in inputs:
        copy.wait()
    pb_send().start()
    packed[...] = jnp.zeros(packed.shape, F32)
    eye = lax.broadcasted_iota(jnp.int32, (R, R), 0) == lax.broadcasted_iota(jnp.int32, (R, R), 1)
    id_column = jnp.sum(jnp.where(eye, ids_ref[...].astype(F32), 0.0), axis=1, keepdims=True)
    packed[0:R, :] = jnp.broadcast_to(id_column, (R, 128))
    packed[R : R + 1, 0:R] = energy[...]
    for k in range(1, Z):
        e_send(k).start()

    def forward(r, last=False):
        for j in range(1, X):
            x_recv(r, j).wait_recv()
            f_send(r, j).start()
        for j in range(1, X):
            x_send(r, j).wait_send()
        if last:
            return
        if isinstance(r, int):
            if r + WINDOW < R:
                start_x(r + WINDOW)
        else:
            pl.when(r + WINDOW < R)(lambda: start_x(r + WINDOW))

    def grads_of(r):
        cot_copy(r).wait()
        act_copy(r).wait()
        b_recv(r).wait_recv()
        for j in range(1, X):
            f_recv(r, j).wait_recv()
        flipped = jnp.dot(cbuf[r], agath[r], preferred_element_type=F32)
        return flipped.T

    def send_row(i):
        rbuf[z, i] = sbuf[i, chunk(z), :]
        for k in range(1, Z):
            z_send(i, k).start()

    def first():
        g = grads_of(0)
        high = g.astype(BF16)
        low = (g - high.astype(F32)).astype(BF16)
        sbuf[0] = high
        sbuf[R] = low
        run[...] = high.astype(F32) + low.astype(F32)
        send_row(0)
        send_row(R)

    def inverse(r):
        return 1.0 / jnp.asarray(r, F32)

    def later(r):
        g = grads_of(r)
        middle = run[...] * inverse(r)
        step = (g - middle).astype(BF16)
        sbuf[r] = step
        run[...] += middle + step.astype(F32)
        send_row(r)

    forward(0)
    forward(1)
    first()

    def body(r, _):
        forward(r)
        later(r - 1)
        return 0

    lax.fori_loop(2, R - 1, body, 0)
    forward(R - 1, last=True)
    for j in range(1, X):
        p_send(j).start()
    later(R - 2)
    later(R - 1)

    stored[p] = prev[chunk(z), :]
    pb_recv().wait_recv()
    for j in range(1, X):
        p_recv(j).wait_recv()
        pf_send(j).start()
    for j in range(1, X):
        pf_recv(j).wait_recv()
    mine = order[:, pl.ds(pl.multiple_of(p * O, O), O)]
    acc = jnp.zeros((3 * dc, O), F32)
    for q in range(PP):
        hot = (lax.broadcasted_iota(jnp.int32, (O, O), 0) + q * O == mine).astype(F32).astype(BF16)
        s = stored[q]
        s1 = s.astype(BF16)
        rest = s - s1.astype(F32)
        s2 = rest.astype(BF16)
        s3 = (rest - s2.astype(F32)).astype(BF16)
        acc += jnp.dot(jnp.concatenate([s1, s2, s3], axis=0), hot, preferred_element_type=F32)
    alig[...] = acc[:dc] + (acc[dc : 2 * dc] + acc[2 * dc :])

    for k in range(1, Z):
        e_recv(k).wait_recv()
    ebuf[z] = packed[...]
    lane = lax.broadcasted_iota(jnp.int32, (R, 128), 1)
    energy_sum = jnp.zeros((1, 1), F32)
    for q in range(Z):
        energy_sum += jnp.sum(ebuf[q, R : R + 1, :], axis=1, keepdims=True)
    energy_mean = energy_sum / W
    for q in range(Z):
        ids = ebuf[q, 0:R, :]
        picked = jnp.zeros((R, 128), F32)
        for s in range(Z):
            hit = (ids == (lane + s * R).astype(F32)) & (lane < R)
            picked += jnp.where(hit, ebuf[s, R : R + 1, :], 0.0)
        value = jnp.sum(picked, axis=1, keepdims=True) - energy_mean
        esort[q * R : (q + 1) * R, :] = jnp.broadcast_to(value, (R, 128))

    for k in range(1, Z):
        z_recv(0, k).wait_recv()
        z_recv(R, k).wait_recv()

    def put(q, r, g):
        for h in range(halves):
            cent[h, pl.ds(pl.multiple_of((q * R + r) * dc, dc), dc), :] = g[:, h * 128 : (h + 1) * 128]

    for q in range(Z):
        g = rbuf[q, 0].astype(F32) + rbuf[q, R].astype(F32)
        runs[q] = g
        put(q, 0, g)

    def rebuild(r, _):
        for k in range(1, Z):
            z_recv(r, k).wait_recv()
        for q in range(Z):
            middle = runs[q] * inverse(r)
            g = middle + rbuf[q, r].astype(F32)
            put(q, r, g)
            runs[q] += g
        return 0

    lax.fori_loop(1, R, rebuild, 0)
    acc = runs[0]
    for q in range(1, Z):
        acc += runs[q]
    mean_ref[...] = acc * (1.0 / W)

    def gram_step(i, carry):
        gram, proj = carry
        parts = []
        for u in range(4):
            d = i * 4 + u
            row = jnp.concatenate(
                [cent[h, pl.ds(d, W, stride=dc), :] for h in range(halves)], axis=1
            )
            row = row - mean_ref[pl.ds(d, 1), :]
            proj = proj + row * alig[pl.ds(d, 1), :]
            parts.append(row.astype(BF16))
        wide = jnp.concatenate(parts, axis=1)
        gram = gram + lax.dot_general(
            wide, wide, (((1,), (1,)), ((), ())), preferred_element_type=F32
        )
        return gram, proj

    gram, proj = lax.fori_loop(
        0, dc // 4, gram_step, (jnp.zeros((W, W), F32), jnp.zeros((W, O), F32))
    )
    whole = jnp.concatenate(
        [gram, jnp.sum(proj, axis=1, keepdims=True), jnp.zeros((W, L - W - 1), F32)], axis=1
    )
    if fold:
        gsum[...] = whole[: W // 2] + pltpu.roll(whole[W // 2 :], L // 2, 1)
    else:
        gsum[...] = whole
    for j in range(1, PP):
        g_send(j).start()
    gred[p] = gsum[...]
    for j in range(1, PP):
        g_recv(j).wait_recv()
    acc = gred[0]
    for q in range(1, PP):
        acc += gred[q]
    zred[z] = acc
    for k in range(1, Z):
        h_send(k).start()
    for k in range(1, Z):
        h_recv(k).wait_recv()
    acc = zred[0]
    for q in range(1, Z):
        acc += zred[q]
    if fold:
        acc = jnp.concatenate([acc, pltpu.roll(acc, L // 2, 1)], axis=0)

    sub = lax.broadcasted_iota(jnp.int32, (W, L), 0)
    col = lax.broadcasted_iota(jnp.int32, (W, L), 1)
    damp = jnp.where(sub == col, 0.002, 0.0) + 1.0 / W
    zeta = esort[:, 0:1] - 0.9 * acc[:, W : W + 1]
    m = jnp.where(col == W, zeta, acc + damp)
    for k in range(0, W, 2):
        r0, r1 = m[k : k + 1, :], m[k + 1 : k + 2, :]
        c0, c1 = m[:, k : k + 1], m[:, k + 1 : k + 2]
        up, low = r0[:, k + 1 : k + 2], r1[:, k : k + 1]
        inv0 = 1.0 / r0[:, k : k + 1]
        ratio = up * inv0
        inv1 = 1.0 / (r1[:, k + 1 : k + 2] - low * ratio)
        p1 = (r1 - (low * inv0) * r0) * inv1
        p0 = r0 * inv0 - ratio * p1
        m = jnp.where(sub == k, p0, jnp.where(sub == k + 1, p1, m - c0 * p0 - c1 * p1))
    solved = jnp.broadcast_to(m[:, W : W + 1], (W, 128))
    csol[...] = solved
    sub = lax.broadcasted_iota(jnp.int32, (W, 128), 0)
    col = lax.broadcasted_iota(jnp.int32, (W, 128), 1)
    coef_out[...] = jnp.sum(jnp.where(sub == col + z * R, solved, 0.0), axis=0, keepdims=True)

    for h in range(halves):
        cols = slice(h * 128, (h + 1) * 128)
        mean_half = mean_ref[:, cols]

        def add(w, acc):
            part = cent[h, pl.ds(pl.multiple_of(w * dc, dc), dc), :] - mean_half
            return acc + csol[pl.ds(w, 1), :] * part

        acc = lax.fori_loop(0, W, add, jnp.zeros((dc, 128), F32), unroll=4)
        dscr[chunk(z), cols] = acc + 0.9 * alig[:, cols]
    for k in range(1, Z):
        d_send(k).start()
    for k in range(1, Z):
        d_recv(k).wait_recv()
    dir_out[...] = dscr[...]

    def drain(r, _):
        for j in range(1, X):
            f_send(r, j).wait_send()
        b_send(r).wait_send()
        return 0

    lax.fori_loop(0, R, drain, 0)

    def drain_rows(i, _):
        for k in range(1, Z):
            z_send(i, k).wait_send()
        return 0

    lax.fori_loop(0, R + 1, drain_rows, 0)
    for j in range(1, PP):
        g_send(j).wait_send()
    pb_send().wait_send()
    for j in range(1, X):
        p_send(j).wait_send()
        pf_send(j).wait_send()
    for k in range(1, Z):
        e_send(k).wait_send()
        h_send(k).wait_send()
        d_send(k).wait_send()


def fused_shards(
    activations, cotangents, local_energy, walker_ids, prev_direction, column_order, weights
):
    R, n, D = activations.shape
    O, N = cotangents.shape[1:]
    Z = lax.axis_size("walker")
    PP = lax.axis_size("param")
    X = PP // 2
    W = R * Z
    dc = D // Z
    L = -(-(W + 1) // 128) * 128
    rp = -(-(R + 1) // 8) * 8
    grows = W // 2 if L == 128 and W + 1 <= 64 and W % 16 == 0 else W
    vmem = pl.BlockSpec(memory_space=pltpu.VMEM)
    hbm = pl.BlockSpec(memory_space=pltpu.HBM)
    dma = pltpu.SemaphoreType.DMA
    direction, coef = pl.pallas_call(
        functools.partial(kernel, Z=Z, PP=PP),
        out_shape=(
            jax.ShapeDtypeStruct((D, O), F32),
            jax.ShapeDtypeStruct((1, 128), F32),
        ),
        in_specs=[hbm] * 6,
        out_specs=(vmem, vmem),
        scratch_shapes=[
            pltpu.VMEM((R, N, D), BF16),
            pltpu.VMEM((R, O, N), BF16),
            pltpu.VMEM((R + 1, D, O), BF16),
            pltpu.VMEM((Z, R + 1, dc, O), BF16),
            pltpu.VMEM((D, O), F32),
            pltpu.VMEM((Z, dc, O), F32),
            pltpu.VMEM((dc, O), F32),
            pltpu.VMEM((O // 128, W * dc, 128), F32),
            pltpu.VMEM((PP, dc, O), F32),
            pltpu.VMEM((dc, O), F32),
            pltpu.VMEM((dc, O), F32),
            pltpu.VMEM((PP, grows, L), F32),
            pltpu.VMEM((Z, grows, L), F32),
            pltpu.VMEM((grows, L), F32),
            pltpu.VMEM((D, O), F32),
            pltpu.VMEM((Z, rp, 128), F32),
            pltpu.VMEM((W, 128), F32),
            pltpu.VMEM((W, 128), F32),
            pltpu.VMEM((D, O), F32),
            pltpu.VMEM((1, O * PP), jnp.int32),
            pltpu.VMEM((1, R), F32),
            pltpu.VMEM((1, R), jnp.int32),
            pltpu.VMEM((rp, 128), F32),
            dma((2, R)),
            dma((4,)),
            dma((R, X)), dma((R, X)),
            dma((R,)), dma((R,)),
            dma((R, X)), dma((R, X)),
            dma((R + 1, Z)), dma((R + 1, Z)),
            dma((X,)), dma((X,)),
            dma((1,)), dma((1,)),
            dma((X,)), dma((X,)),
            dma((PP,)), dma((PP,)),
            dma((Z,)), dma((Z,)),
            dma((Z,)), dma((Z,)),
            dma((Z,)), dma((Z,)),
        ],
        compiler_params=pltpu.CompilerParams(
            collective_id=0, has_side_effects=True, vmem_limit_bytes=60 * 1024 * 1024
        ),
        cost_estimate=pl.CostEstimate(
            flops=2 * R * D * O * N, bytes_accessed=2 * R * N * (D + O), transcendentals=0
        ),
    )(
        activations, cotangents, prev_direction, column_order.reshape(1, -1),
        local_energy.reshape(1, -1), walker_ids.reshape(1, -1),
    )

    def finish(d_ref, c_ref, w_ref, dir_ref, new_ref, mine_ref):
        value = d_ref[...]
        dir_ref[...] = value
        new_ref[...] = w_ref[...] - 0.05 * value
        mine_ref[...] = c_ref[:, 0:R]

    direction, new_weights, mine = pl.pallas_call(
        finish,
        out_shape=(
            jax.ShapeDtypeStruct((D, O), F32),
            jax.ShapeDtypeStruct((D, O), F32),
            jax.ShapeDtypeStruct((1, R), F32),
        ),
        in_specs=[vmem] * 3,
        out_specs=(vmem, vmem, vmem),
    )(direction, coef, weights)
    return (direction, new_weights, mine.reshape(-1))


def shards(*args):
    R, n, D = args[0].shape
    O = args[1].shape[1]
    Z = lax.axis_size("walker")
    fits = O % 128 == 0 and D % (16 * Z) == 0 and R * Z <= 120 and R >= 4 and R * Z % 2 == 0 and n % 16 == 0
    if fits and lax.axis_size("param") % 2 == 0:
        return fused_shards(*args)
    return plain_shards(*args)


def solution(mesh):
    in_specs = (
        P(("group", "walker"), "param", None),
        P(("group", "walker"), "param", None),
        P(("group", "walker")),
        P(("group", "walker")),
        P("group", "param"),
        P("group"),
        P("group", "param"),
    )
    out_specs = (P("group", "param"), P("group", "param"), P(("group", "walker")))
    return jax.shard_map(shards, mesh=mesh, in_specs=in_specs, out_specs=out_specs, check_vma=False)
```

```python
import functools

import jax
import jax.numpy as jnp
from jax import lax
from jax.experimental import pallas as pl
from jax.experimental.pallas import tpu as pltpu
from jax.sharding import PartitionSpec as P

F32 = jnp.float32
BF16 = jnp.bfloat16
MESH = pl.DeviceIdType.MESH
WINDOW = 3


def solve_system(system, zeta):
    factor = jnp.linalg.cholesky(system)
    column = zeta[:, None]
    middle = lax.linalg.triangular_solve(
        factor, column, left_side=True, lower=True, transpose_a=False
    )
    result = lax.linalg.triangular_solve(
        factor, middle, left_side=True, lower=True, transpose_a=True
    )
    return result[:, 0]


def plain_shards(
    activations, cotangents, local_energy, walker_ids, prev_direction, column_order, weights
):
    rows = cotangents.shape[0]
    orb_local = cotangents.shape[1]
    width_in = activations.shape[2]
    walkers = rows * lax.axis_size("walker")
    walker_pos = lax.axis_index("walker")
    param_pos = lax.axis_index("param")
    grads = jnp.einsum(
        "wnd,won->wdo",
        lax.all_gather(activations, "param", axis=1, tiled=True),
        cotangents,
        preferred_element_type=jnp.float32,
    )
    flat = grads.reshape(rows, width_in * orb_local)
    column_total = lax.psum(jnp.sum(flat, axis=0), "walker")
    centered = (flat - column_total / walkers).astype(jnp.bfloat16)
    energies_all = lax.all_gather(local_energy, "walker", axis=0, tiled=True)
    energy_mean = jnp.mean(energies_all)
    centered_energy = energies_all[walker_ids] - energy_mean
    stored = lax.all_gather(prev_direction, "param", axis=1, tiled=True)
    my_order = lax.dynamic_slice_in_dim(column_order, param_pos * orb_local, orb_local)
    aligned = jnp.take(stored, my_order, axis=1)
    wide = centered.astype(jnp.float32)
    proj_part = jnp.dot(wide, aligned.reshape(-1), precision=lax.Precision.HIGHEST)
    block = lax.dot_general(
        centered,
        lax.all_gather(centered, "walker", axis=0, tiled=True),
        (((1,), (1,)), ((), ())),
        preferred_element_type=jnp.float32,
    )
    gram_mine, proj_mine = lax.psum((block, proj_part), "param")
    zeta_mine = centered_energy - 0.9 * proj_mine
    gram, zeta = (
        lax.all_gather(gram_mine, "walker", axis=0, tiled=True),
        lax.all_gather(zeta_mine, "walker", axis=0, tiled=True),
    )
    system = gram + 0.002 * jnp.eye(walkers, dtype=jnp.float32) + 1.0 / walkers
    solved = solve_system(system, zeta)
    mine = lax.dynamic_slice_in_dim(solved, walker_pos * rows, rows)
    update_part = jnp.dot(mine, wide, precision=lax.Precision.HIGHEST)
    update_total = lax.psum(update_part, "walker")
    direction = update_total.reshape(width_in, orb_local) + 0.9 * aligned
    return (direction, weights - 0.05 * direction, mine)


def kernel(
    act, cot, prev_in, order_in, energy_in, ids_in,
    dir_out, coef_out,
    agath, cbuf, sbuf, rbuf, run, runs, total, cent, stored, alig, mean_ref,
    gred, zred, gsum, dscr, ebuf, esort, csol, prev, order, energy, ids_ref, packed,
    loc_sem, in_sem, xs, xr, bs, br, fs, fr, zs, zr, ps, pr, pbs, pbr, pfs, pfr, gs, gr, hs, hr, ds, dr, es, er,
    *, Z, PP,
):
    R, n, D = act.shape
    O = cot.shape[1]
    W = R * Z
    X = PP // 2
    dc = D // Z
    L = gsum.shape[1]
    fold = gsum.shape[0] != W
    halves = O // 128
    z = lax.axis_index("walker")
    p = lax.axis_index("param")
    x = p // 2
    c = p % 2
    sib = x * 2 + (1 - c)

    def xpeer(j):
        return lax.rem(x + j, X) * 2 + c

    def remote(src, dst, ssem, rsem, axis, idx):
        return pltpu.make_async_remote_copy(
            src_ref=src, dst_ref=dst, send_sem=ssem, recv_sem=rsem,
            device_id={axis: idx}, device_id_type=MESH,
        )

    def cot_copy(r):
        return pltpu.make_async_copy(cot.at[r], cbuf.at[r], loc_sem.at[0, r])

    def act_copy(r):
        return pltpu.make_async_copy(
            act.at[r], agath.at[r, pl.ds(pl.multiple_of(p * n, n), n)], loc_sem.at[1, r]
        )

    def rows_of(q):
        return pl.ds(pl.multiple_of(q * n, n), n)

    def x_send(r, j):
        return remote(act.at[r], agath.at[r, rows_of(p)], xs.at[r, j], xr.at[r, x], "param", xpeer(j))

    def x_recv(r, j):
        q = xpeer(j)
        return remote(act.at[r], agath.at[r, rows_of(q)], xs.at[r, j], xr.at[r, q // 2], "param", q)

    def b_send(r):
        return remote(act.at[r], agath.at[r, rows_of(p)], bs.at[r], br.at[r], "param", sib)

    def b_recv(r):
        return remote(act.at[r], agath.at[r, rows_of(sib)], bs.at[r], br.at[r], "param", sib)

    def f_send(r, j):
        q = xpeer(j)
        return remote(
            agath.at[r, rows_of(q)], agath.at[r, rows_of(q)], fs.at[r, j], fr.at[r, j], "param", sib
        )

    def f_recv(r, j):
        q = lax.rem(x + j, X) * 2 + (1 - c)
        return remote(
            agath.at[r, rows_of(q)], agath.at[r, rows_of(q)], fs.at[r, j], fr.at[r, j], "param", sib
        )

    def chunk(q):
        return pl.ds(pl.multiple_of(q * dc, dc), dc)

    def z_send(i, k):
        q = lax.rem(z + k, Z)
        return remote(sbuf.at[i, chunk(q)], rbuf.at[z, i], zs.at[i, k], zr.at[i, z], "walker", q)

    def z_recv(i, k):
        q = lax.rem(z + k, Z)
        return remote(sbuf.at[i, chunk(q)], rbuf.at[q, i], zs.at[i, k], zr.at[i, q], "walker", q)

    def p_send(j):
        return remote(prev.at[chunk(z)], stored.at[p], ps.at[j], pr.at[x], "param", xpeer(j))

    def p_recv(j):
        q = xpeer(j)
        return remote(prev.at[chunk(z)], stored.at[q], ps.at[j], pr.at[q // 2], "param", q)

    def pb_send():
        return remote(prev.at[chunk(z)], stored.at[p], pbs.at[0], pbr.at[0], "param", sib)

    def pb_recv():
        return remote(prev.at[chunk(z)], stored.at[sib], pbs.at[0], pbr.at[0], "param", sib)

    def pf_send(j):
        q = xpeer(j)
        return remote(stored.at[q], stored.at[q], pfs.at[j], pfr.at[j], "param", sib)

    def pf_recv(j):
        q = lax.rem(x + j, X) * 2 + (1 - c)
        return remote(stored.at[q], stored.at[q], pfs.at[j], pfr.at[j], "param", sib)

    def g_send(j):
        q = lax.rem(p + j, PP)
        return remote(gsum, gred.at[p], gs.at[j], gr.at[p], "param", q)

    def g_recv(j):
        q = lax.rem(p + j, PP)
        return remote(gsum, gred.at[q], gs.at[j], gr.at[q], "param", q)

    def h_send(k):
        q = lax.rem(z + k, Z)
        return remote(zred.at[z], zred.at[z], hs.at[k], hr.at[z], "walker", q)

    def h_recv(k):
        q = lax.rem(z + k, Z)
        return remote(zred.at[q], zred.at[q], hs.at[k], hr.at[q], "walker", q)

    def d_send(k):
        q = lax.rem(z + k, Z)
        return remote(dscr.at[chunk(z)], dscr.at[chunk(z)], ds.at[k], dr.at[z], "walker", q)

    def d_recv(k):
        q = lax.rem(z + k, Z)
        return remote(dscr.at[chunk(q)], dscr.at[chunk(q)], ds.at[k], dr.at[q], "walker", q)

    def e_send(k):
        q = lax.rem(z + k, Z)
        return remote(packed, ebuf.at[z], es.at[k], er.at[z], "walker", q)

    def e_recv(k):
        q = lax.rem(z + k, Z)
        return remote(packed, ebuf.at[q], es.at[k], er.at[q], "walker", q)

    barrier = pltpu.get_barrier_semaphore()
    for j in range(1, PP):
        pl.semaphore_signal(barrier, inc=1, device_id={"param": lax.rem(p + j, PP)}, device_id_type=MESH)
    for k in range(1, Z):
        pl.semaphore_signal(barrier, inc=1, device_id={"walker": lax.rem(z + k, Z)}, device_id_type=MESH)

    inputs = [
        pltpu.make_async_copy(src, dst, in_sem.at[i])
        for i, (src, dst) in enumerate(
            ((prev_in, prev), (order_in, order), (energy_in, energy), (ids_in, ids_ref))
        )
    ]
    for copy in inputs:
        copy.start()

    def start_local(r, _):
        cot_copy(r).start()
        act_copy(r).start()
        return 0

    lax.fori_loop(0, R, start_local, 0)
    pl.semaphore_wait(barrier, PP + Z - 2)

    def start_x(r):
        for j in range(1, X):
            x_send(r, j).start()

    for r in range(WINDOW):
        start_x(r)

    def start_b(r, _):
        b_send(r).start()
        return 0

    lax.fori_loop(0, R, start_b, 0)
    for copy in inputs:
        copy.wait()
    pb_send().start()
    packed[...] = jnp.zeros(packed.shape, F32)
    eye = lax.broadcasted_iota(jnp.int32, (R, R), 0) == lax.broadcasted_iota(jnp.int32, (R, R), 1)
    id_column = jnp.sum(jnp.where(eye, ids_ref[...].astype(F32), 0.0), axis=1, keepdims=True)
    packed[0:R, :] = jnp.broadcast_to(id_column, (R, 128))
    packed[R : R + 1, 0:R] = energy[...]
    for k in range(1, Z):
        e_send(k).start()

    def forward(r, last=False):
        for j in range(1, X):
            x_recv(r, j).wait_recv()
            f_send(r, j).start()
        for j in range(1, X):
            x_send(r, j).wait_send()
        if last:
            return
        if isinstance(r, int):
            if r + WINDOW < R:
                start_x(r + WINDOW)
        else:
            pl.when(r + WINDOW < R)(lambda: start_x(r + WINDOW))

    def grads_of(r):
        cot_copy(r).wait()
        act_copy(r).wait()
        b_recv(r).wait_recv()
        for j in range(1, X):
            f_recv(r, j).wait_recv()
        flipped = jnp.dot(cbuf[r], agath[r], preferred_element_type=F32)
        return flipped.T

    def send_row(i):
        rbuf[z, i] = sbuf[i, chunk(z), :]
        for k in range(1, Z):
            z_send(i, k).start()

    def first():
        g = grads_of(0)
        high = g.astype(BF16)
        low = (g - high.astype(F32)).astype(BF16)
        sbuf[0] = high
        sbuf[R] = low
        run[...] = high.astype(F32) + low.astype(F32)
        send_row(0)
        send_row(R)

    def inverse(r):
        return 1.0 / jnp.asarray(r, F32)

    def later(r):
        g = grads_of(r)
        middle = run[...] * inverse(r)
        step = (g - middle).astype(BF16)
        sbuf[r] = step
        run[...] += middle + step.astype(F32)
        send_row(r)

    forward(0)
    first()

    def body(r, _):
        forward(r)
        later(r)
        return 0

    lax.fori_loop(1, R - 1, body, 0)
    forward(R - 1, last=True)
    for j in range(1, X):
        p_send(j).start()
    later(R - 1)

    stored[p] = prev[chunk(z), :]
    pb_recv().wait_recv()
    for j in range(1, X):
        p_recv(j).wait_recv()
        pf_send(j).start()
    for j in range(1, X):
        pf_recv(j).wait_recv()
    mine = order[:, pl.ds(pl.multiple_of(p * O, O), O)]
    acc = jnp.zeros((3 * dc, O), F32)
    for q in range(PP):
        hot = (lax.broadcasted_iota(jnp.int32, (O, O), 0) + q * O == mine).astype(F32).astype(BF16)
        s = stored[q]
        s1 = s.astype(BF16)
        rest = s - s1.astype(F32)
        s2 = rest.astype(BF16)
        s3 = (rest - s2.astype(F32)).astype(BF16)
        acc += jnp.dot(jnp.concatenate([s1, s2, s3], axis=0), hot, preferred_element_type=F32)
    alig[...] = acc[:dc] + (acc[dc : 2 * dc] + acc[2 * dc :])

    for k in range(1, Z):
        e_recv(k).wait_recv()
    ebuf[z] = packed[...]
    lane = lax.broadcasted_iota(jnp.int32, (R, 128), 1)
    energy_sum = jnp.zeros((1, 1), F32)
    for q in range(Z):
        energy_sum += jnp.sum(ebuf[q, R : R + 1, :], axis=1, keepdims=True)
    energy_mean = energy_sum / W
    for q in range(Z):
        ids = ebuf[q, 0:R, :]
        picked = jnp.zeros((R, 128), F32)
        for s in range(Z):
            hit = (ids == (lane + s * R).astype(F32)) & (lane < R)
            picked += jnp.where(hit, ebuf[s, R : R + 1, :], 0.0)
        value = jnp.sum(picked, axis=1, keepdims=True) - energy_mean
        esort[q * R : (q + 1) * R, :] = jnp.broadcast_to(value, (R, 128))

    for k in range(1, Z):
        z_recv(0, k).wait_recv()
        z_recv(R, k).wait_recv()

    def put(q, r, g):
        for h in range(halves):
            cent[h, pl.ds(pl.multiple_of((q * R + r) * dc, dc), dc), :] = g[:, h * 128 : (h + 1) * 128]

    for q in range(Z):
        g = rbuf[q, 0].astype(F32) + rbuf[q, R].astype(F32)
        runs[q] = g
        put(q, 0, g)

    def rebuild(r, _):
        for k in range(1, Z):
            z_recv(r, k).wait_recv()
        for q in range(Z):
            middle = runs[q] * inverse(r)
            g = middle + rbuf[q, r].astype(F32)
            put(q, r, g)
            runs[q] += g
        return 0

    lax.fori_loop(1, R, rebuild, 0)
    acc = runs[0]
    for q in range(1, Z):
        acc += runs[q]
    mean_ref[...] = acc * (1.0 / W)

    def gram_step(i, carry):
        gram, proj = carry
        parts = []
        for u in range(4):
            d = i * 4 + u
            row = jnp.concatenate(
                [cent[h, pl.ds(d, W, stride=dc), :] for h in range(halves)], axis=1
            )
            row = row - mean_ref[pl.ds(d, 1), :]
            proj = proj + row * alig[pl.ds(d, 1), :]
            parts.append(row.astype(BF16))
        wide = jnp.concatenate(parts, axis=1)
        gram = gram + lax.dot_general(
            wide, wide, (((1,), (1,)), ((), ())), preferred_element_type=F32
        )
        return gram, proj

    gram, proj = lax.fori_loop(
        0, dc // 4, gram_step, (jnp.zeros((W, W), F32), jnp.zeros((W, O), F32))
    )
    whole = jnp.concatenate(
        [gram, jnp.sum(proj, axis=1, keepdims=True), jnp.zeros((W, L - W - 1), F32)], axis=1
    )
    if fold:
        gsum[...] = whole[: W // 2] + pltpu.roll(whole[W // 2 :], L // 2, 1)
    else:
        gsum[...] = whole
    for j in range(1, PP):
        g_send(j).start()
    gred[p] = gsum[...]
    for j in range(1, PP):
        g_recv(j).wait_recv()
    acc = gred[0]
    for q in range(1, PP):
        acc += gred[q]
    zred[z] = acc
    for k in range(1, Z):
        h_send(k).start()
    for k in range(1, Z):
        h_recv(k).wait_recv()
    acc = zred[0]
    for q in range(1, Z):
        acc += zred[q]
    if fold:
        acc = jnp.concatenate([acc, pltpu.roll(acc, L // 2, 1)], axis=0)

    sub = lax.broadcasted_iota(jnp.int32, (W, L), 0)
    col = lax.broadcasted_iota(jnp.int32, (W, L), 1)
    damp = jnp.where(sub == col, 0.002, 0.0) + 1.0 / W
    zeta = esort[:, 0:1] - 0.9 * acc[:, W : W + 1]
    m = jnp.where(col == W, zeta, acc + damp)
    for k in range(W):
        pivot_row = m[k : k + 1, :]
        pivot_row = pivot_row / pivot_row[:, k : k + 1]
        m = jnp.where(sub == k, pivot_row, m - m[:, k : k + 1] * pivot_row)
    solved = jnp.broadcast_to(m[:, W : W + 1], (W, 128))
    csol[...] = solved
    sub = lax.broadcasted_iota(jnp.int32, (W, 128), 0)
    col = lax.broadcasted_iota(jnp.int32, (W, 128), 1)
    coef_out[...] = jnp.sum(jnp.where(sub == col + z * R, solved, 0.0), axis=0, keepdims=True)

    for h in range(halves):
        cols = slice(h * 128, (h + 1) * 128)
        mean_half = mean_ref[:, cols]

        def add(w, acc):
            part = cent[h, pl.ds(pl.multiple_of(w * dc, dc), dc), :] - mean_half
            return acc + csol[pl.ds(w, 1), :] * part

        acc = lax.fori_loop(0, W, add, jnp.zeros((dc, 128), F32), unroll=4)
        dscr[chunk(z), cols] = acc + 0.9 * alig[:, cols]
    for k in range(1, Z):
        d_send(k).start()
    for k in range(1, Z):
        d_recv(k).wait_recv()
    dir_out[...] = dscr[...]

    def drain(r, _):
        for j in range(1, X):
            f_send(r, j).wait_send()
        b_send(r).wait_send()
        return 0

    lax.fori_loop(0, R, drain, 0)

    def drain_rows(i, _):
        for k in range(1, Z):
            z_send(i, k).wait_send()
        return 0

    lax.fori_loop(0, R + 1, drain_rows, 0)
    for j in range(1, PP):
        g_send(j).wait_send()
    pb_send().wait_send()
    for j in range(1, X):
        p_send(j).wait_send()
        pf_send(j).wait_send()
    for k in range(1, Z):
        e_send(k).wait_send()
        h_send(k).wait_send()
        d_send(k).wait_send()


def fused_shards(
    activations, cotangents, local_energy, walker_ids, prev_direction, column_order, weights
):
    R, n, D = activations.shape
    O, N = cotangents.shape[1:]
    Z = lax.axis_size("walker")
    PP = lax.axis_size("param")
    X = PP // 2
    W = R * Z
    dc = D // Z
    L = -(-(W + 1) // 128) * 128
    rp = -(-(R + 1) // 8) * 8
    grows = W // 2 if L == 128 and W + 1 <= 64 and W % 16 == 0 else W
    vmem = pl.BlockSpec(memory_space=pltpu.VMEM)
    hbm = pl.BlockSpec(memory_space=pltpu.HBM)
    dma = pltpu.SemaphoreType.DMA
    direction, coef = pl.pallas_call(
        functools.partial(kernel, Z=Z, PP=PP),
        out_shape=(
            jax.ShapeDtypeStruct((D, O), F32),
            jax.ShapeDtypeStruct((1, 128), F32),
        ),
        in_specs=[hbm] * 6,
        out_specs=(vmem, vmem),
        scratch_shapes=[
            pltpu.VMEM((R, N, D), BF16),
            pltpu.VMEM((R, O, N), BF16),
            pltpu.VMEM((R + 1, D, O), BF16),
            pltpu.VMEM((Z, R + 1, dc, O), BF16),
            pltpu.VMEM((D, O), F32),
            pltpu.VMEM((Z, dc, O), F32),
            pltpu.VMEM((dc, O), F32),
            pltpu.VMEM((O // 128, W * dc, 128), F32),
            pltpu.VMEM((PP, dc, O), F32),
            pltpu.VMEM((dc, O), F32),
            pltpu.VMEM((dc, O), F32),
            pltpu.VMEM((PP, grows, L), F32),
            pltpu.VMEM((Z, grows, L), F32),
            pltpu.VMEM((grows, L), F32),
            pltpu.VMEM((D, O), F32),
            pltpu.VMEM((Z, rp, 128), F32),
            pltpu.VMEM((W, 128), F32),
            pltpu.VMEM((W, 128), F32),
            pltpu.VMEM((D, O), F32),
            pltpu.VMEM((1, O * PP), jnp.int32),
            pltpu.VMEM((1, R), F32),
            pltpu.VMEM((1, R), jnp.int32),
            pltpu.VMEM((rp, 128), F32),
            dma((2, R)),
            dma((4,)),
            dma((R, X)), dma((R, X)),
            dma((R,)), dma((R,)),
            dma((R, X)), dma((R, X)),
            dma((R + 1, Z)), dma((R + 1, Z)),
            dma((X,)), dma((X,)),
            dma((1,)), dma((1,)),
            dma((X,)), dma((X,)),
            dma((PP,)), dma((PP,)),
            dma((Z,)), dma((Z,)),
            dma((Z,)), dma((Z,)),
            dma((Z,)), dma((Z,)),
        ],
        compiler_params=pltpu.CompilerParams(
            collective_id=0, has_side_effects=True, vmem_limit_bytes=60 * 1024 * 1024
        ),
        cost_estimate=pl.CostEstimate(
            flops=2 * R * D * O * N, bytes_accessed=2 * R * N * (D + O), transcendentals=0
        ),
    )(
        activations, cotangents, prev_direction, column_order.reshape(1, -1),
        local_energy.reshape(1, -1), walker_ids.reshape(1, -1),
    )

    def finish(d_ref, c_ref, w_ref, dir_ref, new_ref, mine_ref):
        value = d_ref[...]
        dir_ref[...] = value
        new_ref[...] = w_ref[...] - 0.05 * value
        mine_ref[...] = c_ref[:, 0:R]

    direction, new_weights, mine = pl.pallas_call(
        finish,
        out_shape=(
            jax.ShapeDtypeStruct((D, O), F32),
            jax.ShapeDtypeStruct((D, O), F32),
            jax.ShapeDtypeStruct((1, R), F32),
        ),
        in_specs=[vmem] * 3,
        out_specs=(vmem, vmem, vmem),
    )(direction, coef, weights)
    return (direction, new_weights, mine.reshape(-1))


def shards(*args):
    R, n, D = args[0].shape
    O = args[1].shape[1]
    Z = lax.axis_size("walker")
    fits = O % 128 == 0 and D % (16 * Z) == 0 and R * Z <= 120 and R >= 4 and R * Z % 2 == 0 and n % 16 == 0
    if fits and lax.axis_size("param") % 2 == 0:
        return fused_shards(*args)
    return plain_shards(*args)


def solution(mesh):
    in_specs = (
        P(("group", "walker"), "param", None),
        P(("group", "walker"), "param", None),
        P(("group", "walker")),
        P(("group", "walker")),
        P("group", "param"),
        P("group"),
        P("group", "param"),
    )
    out_specs = (P("group", "param"), P("group", "param"), P(("group", "walker")))
    return jax.shard_map(shards, mesh=mesh, in_specs=in_specs, out_specs=out_specs, check_vma=False)
```

```python
import functools

import jax
import jax.numpy as jnp
from jax import lax
from jax.experimental import pallas as pl
from jax.experimental.pallas import tpu as pltpu
from jax.sharding import PartitionSpec as P

F32 = jnp.float32
BF16 = jnp.bfloat16
MESH = pl.DeviceIdType.MESH
WINDOW = 3


def solve_system(system, zeta):
    factor = jnp.linalg.cholesky(system)
    column = zeta[:, None]
    middle = lax.linalg.triangular_solve(
        factor, column, left_side=True, lower=True, transpose_a=False
    )
    result = lax.linalg.triangular_solve(
        factor, middle, left_side=True, lower=True, transpose_a=True
    )
    return result[:, 0]


def plain_shards(
    activations, cotangents, local_energy, walker_ids, prev_direction, column_order, weights
):
    rows = cotangents.shape[0]
    orb_local = cotangents.shape[1]
    width_in = activations.shape[2]
    walkers = rows * lax.axis_size("walker")
    walker_pos = lax.axis_index("walker")
    param_pos = lax.axis_index("param")
    grads = jnp.einsum(
        "wnd,won->wdo",
        lax.all_gather(activations, "param", axis=1, tiled=True),
        cotangents,
        preferred_element_type=jnp.float32,
    )
    flat = grads.reshape(rows, width_in * orb_local)
    column_total = lax.psum(jnp.sum(flat, axis=0), "walker")
    centered = (flat - column_total / walkers).astype(jnp.bfloat16)
    energies_all = lax.all_gather(local_energy, "walker", axis=0, tiled=True)
    energy_mean = jnp.mean(energies_all)
    centered_energy = energies_all[walker_ids] - energy_mean
    stored = lax.all_gather(prev_direction, "param", axis=1, tiled=True)
    my_order = lax.dynamic_slice_in_dim(column_order, param_pos * orb_local, orb_local)
    aligned = jnp.take(stored, my_order, axis=1)
    wide = centered.astype(jnp.float32)
    proj_part = jnp.dot(wide, aligned.reshape(-1), precision=lax.Precision.HIGHEST)
    block = lax.dot_general(
        centered,
        lax.all_gather(centered, "walker", axis=0, tiled=True),
        (((1,), (1,)), ((), ())),
        preferred_element_type=jnp.float32,
    )
    gram_mine, proj_mine = lax.psum((block, proj_part), "param")
    zeta_mine = centered_energy - 0.9 * proj_mine
    gram, zeta = (
        lax.all_gather(gram_mine, "walker", axis=0, tiled=True),
        lax.all_gather(zeta_mine, "walker", axis=0, tiled=True),
    )
    system = gram + 0.002 * jnp.eye(walkers, dtype=jnp.float32) + 1.0 / walkers
    solved = solve_system(system, zeta)
    mine = lax.dynamic_slice_in_dim(solved, walker_pos * rows, rows)
    update_part = jnp.dot(mine, wide, precision=lax.Precision.HIGHEST)
    update_total = lax.psum(update_part, "walker")
    direction = update_total.reshape(width_in, orb_local) + 0.9 * aligned
    return (direction, weights - 0.05 * direction, mine)


def kernel(
    act, cot, prev_in, order_in, energy_in, ids_in,
    dir_out, coef_out,
    agath, cbuf, sbuf, rbuf, run, runs, total, cent, stored, alig, mean_ref,
    gred, zred, gsum, dscr, ebuf, esort, csol, prev, order, energy, ids_ref, packed,
    loc_sem, in_sem, xs, xr, bs, br, fs, fr, zs, zr, ps, pr, pbs, pbr, pfs, pfr, gs, gr, hs, hr, ds, dr, es, er,
    *, Z, PP,
):
    R, n, D = act.shape
    O = cot.shape[1]
    W = R * Z
    X = PP // 2
    dc = D // Z
    L = gsum.shape[1]
    fold = gsum.shape[0] != W
    halves = O // 128
    z = lax.axis_index("walker")
    p = lax.axis_index("param")
    x = p // 2
    c = p % 2
    sib = x * 2 + (1 - c)

    def xpeer(j):
        return lax.rem(x + j, X) * 2 + c

    def remote(src, dst, ssem, rsem, axis, idx):
        return pltpu.make_async_remote_copy(
            src_ref=src, dst_ref=dst, send_sem=ssem, recv_sem=rsem,
            device_id={axis: idx}, device_id_type=MESH,
        )

    def cot_copy(r):
        return pltpu.make_async_copy(cot.at[r], cbuf.at[r], loc_sem.at[0, r])

    def act_copy(r):
        return pltpu.make_async_copy(
            act.at[r], agath.at[r, pl.ds(pl.multiple_of(p * n, n), n)], loc_sem.at[1, r]
        )

    def rows_of(q):
        return pl.ds(pl.multiple_of(q * n, n), n)

    def x_send(r, j):
        return remote(act.at[r], agath.at[r, rows_of(p)], xs.at[r, j], xr.at[r, x], "param", xpeer(j))

    def x_recv(r, j):
        q = xpeer(j)
        return remote(act.at[r], agath.at[r, rows_of(q)], xs.at[r, j], xr.at[r, q // 2], "param", q)

    def b_send(r):
        return remote(act.at[r], agath.at[r, rows_of(p)], bs.at[r], br.at[r], "param", sib)

    def b_recv(r):
        return remote(act.at[r], agath.at[r, rows_of(sib)], bs.at[r], br.at[r], "param", sib)

    def f_send(r, j):
        q = xpeer(j)
        return remote(
            agath.at[r, rows_of(q)], agath.at[r, rows_of(q)], fs.at[r, j], fr.at[r, j], "param", sib
        )

    def f_recv(r, j):
        q = lax.rem(x + j, X) * 2 + (1 - c)
        return remote(
            agath.at[r, rows_of(q)], agath.at[r, rows_of(q)], fs.at[r, j], fr.at[r, j], "param", sib
        )

    def chunk(q):
        return pl.ds(pl.multiple_of(q * dc, dc), dc)

    def z_send(i, k):
        q = lax.rem(z + k, Z)
        return remote(sbuf.at[i, chunk(q)], rbuf.at[z, i], zs.at[i, k], zr.at[i, z], "walker", q)

    def z_recv(i, k):
        q = lax.rem(z + k, Z)
        return remote(sbuf.at[i, chunk(q)], rbuf.at[q, i], zs.at[i, k], zr.at[i, q], "walker", q)

    def p_send(j):
        return remote(prev.at[chunk(z)], stored.at[p], ps.at[j], pr.at[x], "param", xpeer(j))

    def p_recv(j):
        q = xpeer(j)
        return remote(prev.at[chunk(z)], stored.at[q], ps.at[j], pr.at[q // 2], "param", q)

    def pb_send():
        return remote(prev.at[chunk(z)], stored.at[p], pbs.at[0], pbr.at[0], "param", sib)

    def pb_recv():
        return remote(prev.at[chunk(z)], stored.at[sib], pbs.at[0], pbr.at[0], "param", sib)

    def pf_send(j):
        q = xpeer(j)
        return remote(stored.at[q], stored.at[q], pfs.at[j], pfr.at[j], "param", sib)

    def pf_recv(j):
        q = lax.rem(x + j, X) * 2 + (1 - c)
        return remote(stored.at[q], stored.at[q], pfs.at[j], pfr.at[j], "param", sib)

    def g_send(j):
        q = lax.rem(p + j, PP)
        return remote(gsum, gred.at[p], gs.at[j], gr.at[p], "param", q)

    def g_recv(j):
        q = lax.rem(p + j, PP)
        return remote(gsum, gred.at[q], gs.at[j], gr.at[q], "param", q)

    def h_send(k):
        q = lax.rem(z + k, Z)
        return remote(zred.at[z], zred.at[z], hs.at[k], hr.at[z], "walker", q)

    def h_recv(k):
        q = lax.rem(z + k, Z)
        return remote(zred.at[q], zred.at[q], hs.at[k], hr.at[q], "walker", q)

    def d_send(k):
        q = lax.rem(z + k, Z)
        return remote(dscr.at[chunk(z)], dscr.at[chunk(z)], ds.at[k], dr.at[z], "walker", q)

    def d_recv(k):
        q = lax.rem(z + k, Z)
        return remote(dscr.at[chunk(q)], dscr.at[chunk(q)], ds.at[k], dr.at[q], "walker", q)

    def e_send(k):
        q = lax.rem(z + k, Z)
        return remote(packed, ebuf.at[z], es.at[k], er.at[z], "walker", q)

    def e_recv(k):
        q = lax.rem(z + k, Z)
        return remote(packed, ebuf.at[q], es.at[k], er.at[q], "walker", q)

    barrier = pltpu.get_barrier_semaphore()
    for j in range(1, PP):
        pl.semaphore_signal(barrier, inc=1, device_id={"param": lax.rem(p + j, PP)}, device_id_type=MESH)
    for k in range(1, Z):
        pl.semaphore_signal(barrier, inc=1, device_id={"walker": lax.rem(z + k, Z)}, device_id_type=MESH)

    inputs = [
        pltpu.make_async_copy(src, dst, in_sem.at[i])
        for i, (src, dst) in enumerate(
            ((prev_in, prev), (order_in, order), (energy_in, energy), (ids_in, ids_ref))
        )
    ]
    for copy in inputs:
        copy.start()

    def start_local(r, _):
        cot_copy(r).start()
        act_copy(r).start()
        return 0

    lax.fori_loop(0, R, start_local, 0)
    pl.semaphore_wait(barrier, PP + Z - 2)

    def start_x(r):
        for j in range(1, X):
            x_send(r, j).start()

    for r in range(WINDOW):
        start_x(r)

    def start_b(r, _):
        b_send(r).start()
        return 0

    lax.fori_loop(0, R, start_b, 0)
    for copy in inputs:
        copy.wait()
    pb_send().start()
    packed[...] = jnp.zeros(packed.shape, F32)
    eye = lax.broadcasted_iota(jnp.int32, (R, R), 0) == lax.broadcasted_iota(jnp.int32, (R, R), 1)
    id_column = jnp.sum(jnp.where(eye, ids_ref[...].astype(F32), 0.0), axis=1, keepdims=True)
    packed[0:R, :] = jnp.broadcast_to(id_column, (R, 128))
    packed[R : R + 1, 0:R] = energy[...]
    for k in range(1, Z):
        e_send(k).start()

    def forward(r, last=False):
        for j in range(1, X):
            x_recv(r, j).wait_recv()
            f_send(r, j).start()
        for j in range(1, X):
            x_send(r, j).wait_send()
        if last:
            return
        if isinstance(r, int):
            if r + WINDOW < R:
                start_x(r + WINDOW)
        else:
            pl.when(r + WINDOW < R)(lambda: start_x(r + WINDOW))

    def grads_of(r):
        cot_copy(r).wait()
        act_copy(r).wait()
        b_recv(r).wait_recv()
        for j in range(1, X):
            f_recv(r, j).wait_recv()
        flipped = jnp.dot(cbuf[r], agath[r], preferred_element_type=F32)
        return flipped.T

    def send_row(i):
        rbuf[z, i] = sbuf[i, chunk(z), :]
        for k in range(1, Z):
            z_send(i, k).start()

    def first():
        g = grads_of(0)
        high = g.astype(BF16)
        low = (g - high.astype(F32)).astype(BF16)
        sbuf[0] = high
        sbuf[R] = low
        run[...] = high.astype(F32) + low.astype(F32)
        send_row(0)
        send_row(R)

    def inverse(r):
        return 1.0 / jnp.asarray(r, F32)

    def later(r):
        g = grads_of(r)
        middle = run[...] * inverse(r)
        step = (g - middle).astype(BF16)
        sbuf[r] = step
        run[...] += middle + step.astype(F32)
        send_row(r)

    forward(0)
    first()

    def body(r, _):
        forward(r)
        later(r)
        return 0

    lax.fori_loop(1, R - 1, body, 0)
    forward(R - 1, last=True)
    for j in range(1, X):
        p_send(j).start()
    later(R - 1)

    stored[p] = prev[chunk(z), :]
    pb_recv().wait_recv()
    for j in range(1, X):
        p_recv(j).wait_recv()
        pf_send(j).start()
    for j in range(1, X):
        pf_recv(j).wait_recv()
    mine = order[:, pl.ds(pl.multiple_of(p * O, O), O)]
    acc = jnp.zeros((3 * dc, O), F32)
    for q in range(PP):
        hot = (lax.broadcasted_iota(jnp.int32, (O, O), 0) + q * O == mine).astype(F32).astype(BF16)
        s = stored[q]
        s1 = s.astype(BF16)
        rest = s - s1.astype(F32)
        s2 = rest.astype(BF16)
        s3 = (rest - s2.astype(F32)).astype(BF16)
        acc += jnp.dot(jnp.concatenate([s1, s2, s3], axis=0), hot, preferred_element_type=F32)
    alig[...] = acc[:dc] + (acc[dc : 2 * dc] + acc[2 * dc :])

    for k in range(1, Z):
        e_recv(k).wait_recv()
    ebuf[z] = packed[...]
    lane = lax.broadcasted_iota(jnp.int32, (R, 128), 1)
    energy_sum = jnp.zeros((1, 1), F32)
    for q in range(Z):
        energy_sum += jnp.sum(ebuf[q, R : R + 1, :], axis=1, keepdims=True)
    energy_mean = energy_sum / W
    for q in range(Z):
        ids = ebuf[q, 0:R, :]
        picked = jnp.zeros((R, 128), F32)
        for s in range(Z):
            hit = (ids == (lane + s * R).astype(F32)) & (lane < R)
            picked += jnp.where(hit, ebuf[s, R : R + 1, :], 0.0)
        value = jnp.sum(picked, axis=1, keepdims=True) - energy_mean
        esort[q * R : (q + 1) * R, :] = jnp.broadcast_to(value, (R, 128))

    for k in range(1, Z):
        z_recv(0, k).wait_recv()
        z_recv(R, k).wait_recv()

    def put(q, r, g):
        for h in range(halves):
            cent[h, pl.ds(pl.multiple_of((q * R + r) * dc, dc), dc), :] = g[:, h * 128 : (h + 1) * 128]

    for q in range(Z):
        g = rbuf[q, 0].astype(F32) + rbuf[q, R].astype(F32)
        runs[q] = g
        put(q, 0, g)

    def rebuild(r, _):
        for k in range(1, Z):
            z_recv(r, k).wait_recv()
        for q in range(Z):
            middle = runs[q] * inverse(r)
            g = middle + rbuf[q, r].astype(F32)
            put(q, r, g)
            runs[q] += g
        return 0

    lax.fori_loop(1, R, rebuild, 0)
    acc = runs[0]
    for q in range(1, Z):
        acc += runs[q]
    mean_ref[...] = acc * (1.0 / W)

    def gram_step(i, carry):
        gram, proj = carry
        parts = []
        for u in range(16):
            d = i * 16 + u
            row = jnp.concatenate(
                [cent[h, pl.ds(d, W, stride=dc), :] for h in range(halves)], axis=1
            )
            row = row - mean_ref[pl.ds(d, 1), :]
            proj = proj + row * alig[pl.ds(d, 1), :]
            parts.append(row.astype(BF16))
        wide = jnp.concatenate(parts, axis=1)
        gram = gram + lax.dot_general(
            wide, wide, (((1,), (1,)), ((), ())), preferred_element_type=F32
        )
        return gram, proj

    gram, proj = lax.fori_loop(
        0, dc // 16, gram_step, (jnp.zeros((W, W), F32), jnp.zeros((W, O), F32))
    )
    whole = jnp.concatenate(
        [gram, jnp.sum(proj, axis=1, keepdims=True), jnp.zeros((W, L - W - 1), F32)], axis=1
    )
    if fold:
        gsum[...] = whole[: W // 2] + pltpu.roll(whole[W // 2 :], L // 2, 1)
    else:
        gsum[...] = whole
    for j in range(1, PP):
        g_send(j).start()
    gred[p] = gsum[...]
    for j in range(1, PP):
        g_recv(j).wait_recv()
    acc = gred[0]
    for q in range(1, PP):
        acc += gred[q]
    zred[z] = acc
    for k in range(1, Z):
        h_send(k).start()
    for k in range(1, Z):
        h_recv(k).wait_recv()
    acc = zred[0]
    for q in range(1, Z):
        acc += zred[q]
    if fold:
        acc = jnp.concatenate([acc, pltpu.roll(acc, L // 2, 1)], axis=0)

    sub = lax.broadcasted_iota(jnp.int32, (W, L), 0)
    col = lax.broadcasted_iota(jnp.int32, (W, L), 1)
    damp = jnp.where(sub == col, 0.002, 0.0) + 1.0 / W
    zeta = esort[:, 0:1] - 0.9 * acc[:, W : W + 1]
    m = jnp.where(col == W, zeta, acc + damp)
    for k in range(W):
        pivot_row = m[k : k + 1, :]
        pivot_row = pivot_row / pivot_row[:, k : k + 1]
        m = jnp.where(sub == k, pivot_row, m - m[:, k : k + 1] * pivot_row)
    solved = jnp.broadcast_to(m[:, W : W + 1], (W, 128))
    csol[...] = solved
    sub = lax.broadcasted_iota(jnp.int32, (W, 128), 0)
    col = lax.broadcasted_iota(jnp.int32, (W, 128), 1)
    coef_out[...] = jnp.sum(jnp.where(sub == col + z * R, solved, 0.0), axis=0, keepdims=True)

    for h in range(halves):
        cols = slice(h * 128, (h + 1) * 128)
        mean_half = mean_ref[:, cols]

        def add(w, acc):
            part = cent[h, pl.ds(pl.multiple_of(w * dc, dc), dc), :] - mean_half
            return acc + csol[pl.ds(w, 1), :] * part

        acc = lax.fori_loop(0, W, add, jnp.zeros((dc, 128), F32), unroll=4)
        dscr[chunk(z), cols] = acc + 0.9 * alig[:, cols]
    for k in range(1, Z):
        d_send(k).start()
    for k in range(1, Z):
        d_recv(k).wait_recv()
    dir_out[...] = dscr[...]

    def drain(r, _):
        for j in range(1, X):
            f_send(r, j).wait_send()
        b_send(r).wait_send()
        return 0

    lax.fori_loop(0, R, drain, 0)

    def drain_rows(i, _):
        for k in range(1, Z):
            z_send(i, k).wait_send()
        return 0

    lax.fori_loop(0, R + 1, drain_rows, 0)
    for j in range(1, PP):
        g_send(j).wait_send()
    pb_send().wait_send()
    for j in range(1, X):
        p_send(j).wait_send()
        pf_send(j).wait_send()
    for k in range(1, Z):
        e_send(k).wait_send()
        h_send(k).wait_send()
        d_send(k).wait_send()


def fused_shards(
    activations, cotangents, local_energy, walker_ids, prev_direction, column_order, weights
):
    R, n, D = activations.shape
    O, N = cotangents.shape[1:]
    Z = lax.axis_size("walker")
    PP = lax.axis_size("param")
    X = PP // 2
    W = R * Z
    dc = D // Z
    L = -(-(W + 1) // 128) * 128
    rp = -(-(R + 1) // 8) * 8
    grows = W // 2 if L == 128 and W + 1 <= 64 and W % 16 == 0 else W
    vmem = pl.BlockSpec(memory_space=pltpu.VMEM)
    hbm = pl.BlockSpec(memory_space=pltpu.HBM)
    dma = pltpu.SemaphoreType.DMA
    direction, coef = pl.pallas_call(
        functools.partial(kernel, Z=Z, PP=PP),
        out_shape=(
            jax.ShapeDtypeStruct((D, O), F32),
            jax.ShapeDtypeStruct((1, 128), F32),
        ),
        in_specs=[hbm] * 6,
        out_specs=(vmem, vmem),
        scratch_shapes=[
            pltpu.VMEM((R, N, D), BF16),
            pltpu.VMEM((R, O, N), BF16),
            pltpu.VMEM((R + 1, D, O), BF16),
            pltpu.VMEM((Z, R + 1, dc, O), BF16),
            pltpu.VMEM((D, O), F32),
            pltpu.VMEM((Z, dc, O), F32),
            pltpu.VMEM((dc, O), F32),
            pltpu.VMEM((O // 128, W * dc, 128), F32),
            pltpu.VMEM((PP, dc, O), F32),
            pltpu.VMEM((dc, O), F32),
            pltpu.VMEM((dc, O), F32),
            pltpu.VMEM((PP, grows, L), F32),
            pltpu.VMEM((Z, grows, L), F32),
            pltpu.VMEM((grows, L), F32),
            pltpu.VMEM((D, O), F32),
            pltpu.VMEM((Z, rp, 128), F32),
            pltpu.VMEM((W, 128), F32),
            pltpu.VMEM((W, 128), F32),
            pltpu.VMEM((D, O), F32),
            pltpu.VMEM((1, O * PP), jnp.int32),
            pltpu.VMEM((1, R), F32),
            pltpu.VMEM((1, R), jnp.int32),
            pltpu.VMEM((rp, 128), F32),
            dma((2, R)),
            dma((4,)),
            dma((R, X)), dma((R, X)),
            dma((R,)), dma((R,)),
            dma((R, X)), dma((R, X)),
            dma((R + 1, Z)), dma((R + 1, Z)),
            dma((X,)), dma((X,)),
            dma((1,)), dma((1,)),
            dma((X,)), dma((X,)),
            dma((PP,)), dma((PP,)),
            dma((Z,)), dma((Z,)),
            dma((Z,)), dma((Z,)),
            dma((Z,)), dma((Z,)),
        ],
        compiler_params=pltpu.CompilerParams(
            collective_id=0, has_side_effects=True, vmem_limit_bytes=60 * 1024 * 1024
        ),
        cost_estimate=pl.CostEstimate(
            flops=2 * R * D * O * N, bytes_accessed=2 * R * N * (D + O), transcendentals=0
        ),
    )(
        activations, cotangents, prev_direction, column_order.reshape(1, -1),
        local_energy.reshape(1, -1), walker_ids.reshape(1, -1),
    )

    def finish(d_ref, c_ref, w_ref, dir_ref, new_ref, mine_ref):
        value = d_ref[...]
        dir_ref[...] = value
        new_ref[...] = w_ref[...] - 0.05 * value
        mine_ref[...] = c_ref[:, 0:R]

    direction, new_weights, mine = pl.pallas_call(
        finish,
        out_shape=(
            jax.ShapeDtypeStruct((D, O), F32),
            jax.ShapeDtypeStruct((D, O), F32),
            jax.ShapeDtypeStruct((1, R), F32),
        ),
        in_specs=[vmem] * 3,
        out_specs=(vmem, vmem, vmem),
    )(direction, coef, weights)
    return (direction, new_weights, mine.reshape(-1))


def shards(*args):
    R, n, D = args[0].shape
    O = args[1].shape[1]
    Z = lax.axis_size("walker")
    fits = O % 128 == 0 and D % (16 * Z) == 0 and R * Z <= 120 and R >= 4 and R * Z % 2 == 0 and n % 16 == 0
    if fits and lax.axis_size("param") % 2 == 0:
        return fused_shards(*args)
    return plain_shards(*args)


def solution(mesh):
    in_specs = (
        P(("group", "walker"), "param", None),
        P(("group", "walker"), "param", None),
        P(("group", "walker")),
        P(("group", "walker")),
        P("group", "param"),
        P("group"),
        P("group", "param"),
    )
    out_specs = (P("group", "param"), P("group", "param"), P(("group", "walker")))
    return jax.shard_map(shards, mesh=mesh, in_specs=in_specs, out_specs=out_specs, check_vma=False)
```
